32 devices in a mesh: clips: 2 (over x), segment: 2 (over core), rows: 8 (over z, y).
Axes of the slice: x: 2, y: 2, z: 4, core: 2. Of those that a mesh axis runs over, the one named last changes fastest.
Arguments:
- latent: float32 [4, 48, 512], P('clips', 'rows', 'segment'), parts along dimension 0, may hold values from -6 to 6
- stale: bfloat16 [2, 4, 48, 128, 320], P('segment', 'clips', 'rows'), parts along dimension 1, may hold values from -6 to 6
- timesteps: int32 [4], P('clips'), parts along dimension 0, may hold values from 0 to 999
- w_in: bfloat16 [4, 320], replicated, may hold values from -3 to 3
- w_enc: bfloat16 [3, 3, 320, 320], replicated, may hold values from -0.109375 to 0.109375
- w_down: bfloat16 [3, 3, 320, 640], replicated, may hold values from -0.109375 to 0.109375
- w_tmid: bfloat16 [3, 640, 640], replicated, may hold values from -0.125 to 0.125
- w_up: bfloat16 [640, 320], replicated, may hold values from -0.25 to 0.25
- w_skip: bfloat16 [640, 320], replicated, may hold values from -0.25 to 0.25
- w_dec: bfloat16 [3, 3, 320, 320], replicated, may hold values from -0.109375 to 0.109375
- w_out: bfloat16 [3, 3, 320, 4], replicated, may hold values from -0.109375 to 0.109375
- w_time: bfloat16 [320, 1280], replicated, may hold values from -0.3125 to 0.3125
Outputs:
- next_latent: float32 [4, 48, 512], P('clips', 'rows', 'segment'), parts along dimension 0
- features: bfloat16 [2, 4, 48, 128, 320], P('segment', 'clips', 'rows'), parts along dimension 1
The draws below stay inside these ranges and needn't reach their ends.
There are 2 independent parts, one for each index of `clips`. The reference program is written for one: setup_inputs(seed, part) draws one part's arguments, and reference() takes and returns one part's arrays. A program takes and returns all parts, laid end to end along the dimension named above; an argument that names none is the same for every part. Nothing has to cross between parts.
Inputs may be any that keep to these rules, and one draw needn't show every extreme that they name: `timesteps`: one diffusion timestep index a step.
All inputs are finite; a program needn't handle non-finite values.
Results may differ from the reference program's by a relative error of at most 0.006.
Values may be sent and summed in bfloat16 or wider, within the bound.
A program may use at most 128 MiB of HBM per device.

```python
import math
import jax
import jax.numpy as jnp
from jax import lax

C_ENC = 320
C_MID = 640
LAT = 4
WIDTH_LAT = 128
FRAMES = 2
STEPS = 2
HEIGHT = 48


def shard_levels(key, extent, cuts, low, largest):
    level, own = 1.0, jax.random.fold_in(key, 6)
    for dim, blocks in cuts:
        heights = jnp.exp(jax.random.uniform(jax.random.fold_in(own, dim), (blocks,), jnp.float32, low / len(cuts), largest / len(cuts)))
        level = level * jnp.repeat(heights, extent[dim] // blocks).reshape([-1 if axis == dim else 1 for axis in range(len(extent))])
    return level


def gaussian(stream_key, dims, scale, reach, cuts=(), kind=jnp.bfloat16):
    result = scale * jax.random.normal(stream_key, dims, jnp.float32)
    if cuts:
        result = result * shard_levels(stream_key, dims, cuts, -0.22, 0.18)
    return jnp.clip(result, -reach, reach).astype(kind)


def setup_inputs(seed: int = 0, part: int = 0) -> dict:
    keys = jax.random.split(jax.random.key(seed), 13)
    part_keys = jax.random.split(jax.random.fold_in(keys[12], part), 13)
    latent = gaussian(part_keys[0], (FRAMES, HEIGHT, WIDTH_LAT * LAT), 1.0, 6.0, ((1, 8), (2, 2)), jnp.float32)
    stale = gaussian(part_keys[1], (2, FRAMES, HEIGHT, WIDTH_LAT, C_ENC), 1.0, 6.0, ((0, 2), (2, 8)))
    timesteps = jax.random.randint(part_keys[2], (STEPS,), 0, 1000).astype(jnp.int32)
    w_in = gaussian(keys[3], (LAT, C_ENC), LAT ** -0.5, 3.0)
    w_enc = gaussian(keys[4], (3, 3, C_ENC, C_ENC), (9 * C_ENC) ** -0.5, 0.109375)
    w_down = gaussian(keys[5], (3, 3, C_ENC, C_MID), (9 * C_ENC) ** -0.5, 0.109375)
    w_tmid = gaussian(keys[6], (3, C_MID, C_MID), (3 * C_MID) ** -0.5, 0.125)
    w_up = gaussian(keys[7], (C_MID, C_ENC), C_MID ** -0.5, 0.25)
    w_skip = gaussian(keys[8], (2 * C_ENC, C_ENC), (2 * C_ENC) ** -0.5, 0.25)
    w_dec = gaussian(keys[9], (3, 3, C_ENC, C_ENC), (9 * C_ENC) ** -0.5, 0.109375)
    w_out = gaussian(keys[10], (3, 3, C_ENC, LAT), (9 * C_ENC) ** -0.5, 0.109375)
    w_time = gaussian(keys[11], (C_ENC, 2 * C_ENC + C_MID), C_ENC ** -0.5, 0.3125)
    return {"latent": latent, "stale": stale, "timesteps": timesteps, "w_in": w_in, "w_enc": w_enc, "w_down": w_down, "w_tmid": w_tmid, "w_up": w_up, "w_skip": w_skip, "w_dec": w_dec, "w_out": w_out, "w_time": w_time}


EPSILON = 1e-06

def einsum32(form, left, right):
    return jnp.einsum(form, left.astype(jnp.float32), right.astype(jnp.float32))

def normed(values):
    scale = lax.rsqrt(lax.optimization_barrier(jnp.mean(values * values, axis=-1, keepdims=True)) + EPSILON)
    return jax.nn.silu(values * scale)

def pad_rows(values):
    return jnp.pad(values, ((0, 0), (1, 1), (0, 0), (0, 0)))

def conv_rows(extended, weight, count):
    padded = jnp.pad(extended, ((0, 0), (0, 0), (1, 1), (0, 0)))
    columns = extended.shape[2]
    total = jnp.zeros((extended.shape[0], count, columns, weight.shape[3]), jnp.float32)
    for row_off in range(3):
        for col_off in range(3):
            window = padded[:, row_off:row_off + count, col_off:col_off + columns, :]
            total = total + einsum32('fhwc,co->fhwo', window, weight[row_off, col_off])
    return total

def conv_down(extended, weight, count):
    padded = jnp.pad(extended, ((0, 0), (0, 0), (1, 1), (0, 0)))
    columns = extended.shape[2] // 2
    total = jnp.zeros((extended.shape[0], count, columns, weight.shape[3]), jnp.float32)
    for row_off in range(3):
        for col_off in range(3):
            window = padded[:, row_off:row_off + 2 * count:2, col_off:col_off + 2 * columns:2, :]
            total = total + einsum32('fhwc,co->fhwo', window, weight[row_off, col_off])
    return total

def temporal(values, weight):
    frames = values.shape[0]
    padded = jnp.pad(values, ((1, 1), (0, 0), (0, 0), (0, 0)))
    total = jnp.zeros(values.shape[:3] + (weight.shape[2],), jnp.float32)
    for offset in range(3):
        total = total + einsum32('fhwc,co->fhwo', padded[offset:offset + frames], weight[offset])
    return total

def time_bias(step_time, w_time):
    half = w_time.shape[0] // 2
    freqs = jnp.exp(-math.log(10000.0) * jnp.arange(half).astype(jnp.float32) / half)
    angles = step_time.astype(jnp.float32) * freqs
    embedded = jnp.concatenate([jnp.sin(angles), jnp.cos(angles)])
    gated = jax.nn.silu(embedded).astype(jnp.bfloat16)
    return jnp.dot(gated[None, :], w_time, preferred_element_type=jnp.float32)[0]

def reference(latent, stale, timesteps, w_in, w_enc, w_down, w_tmid, w_up, w_skip, w_dec, w_out, w_time):
    chans = w_enc.shape[3]
    mid_chans = w_down.shape[3]
    current = latent
    enc_map = stale[0]
    mid_map = stale[1]
    for step in range(STEPS):
        biases = time_bias(timesteps[step], w_time)
        bias_enc = biases[:chans]
        bias_mid = biases[chans:chans + mid_chans]
        bias_dec = biases[chans + mid_chans:]
        inputs = current.reshape(FRAMES, HEIGHT, WIDTH_LAT, LAT).astype(jnp.bfloat16)
        lifted = einsum32('fhwc,co->fhwo', inputs, w_in)
        activated = normed(lifted).astype(jnp.bfloat16)
        fresh_enc = (lifted + conv_rows(pad_rows(activated), w_enc, HEIGHT) + bias_enc).astype(jnp.bfloat16)
        gated_enc = normed(enc_map.astype(jnp.float32)).astype(jnp.bfloat16)
        lowered = conv_down(pad_rows(gated_enc), w_down, HEIGHT // 2) + bias_mid
        mixed_time = lowered + temporal(normed(lowered).astype(jnp.bfloat16), w_tmid)
        raised = einsum32('fhwc,co->fhwo', mixed_time.astype(jnp.bfloat16), w_up).astype(jnp.bfloat16)
        fresh_mid = jnp.repeat(jnp.repeat(raised, 2, axis=1), 2, axis=2)
        joined = jnp.concatenate([mid_map, enc_map], axis=-1)
        mixed = einsum32('fhwc,co->fhwo', joined, w_skip)
        gated = normed(mixed).astype(jnp.bfloat16)
        decoded = mixed + conv_rows(pad_rows(gated), w_dec, HEIGHT) + bias_dec
        outlet = normed(decoded).astype(jnp.bfloat16)
        noise = conv_rows(pad_rows(outlet), w_out, HEIGHT)
        coefficient = (timesteps[step].astype(jnp.float32) + 1.0) / 1000.0
        current = current - coefficient * noise.reshape(FRAMES, HEIGHT, WIDTH_LAT * LAT)
        enc_map = fresh_enc
        mid_map = fresh_mid
    return (current, jnp.stack([enc_map, mid_map]))
```

```python
import functools
import math

import jax
import jax.numpy as jnp
from jax import lax
from jax.experimental import pallas as pl
from jax.experimental.pallas import tpu as pltpu
from jax.sharding import PartitionSpec as P

EPSILON = 1e-06
F32 = jnp.float32
BF16 = jnp.bfloat16
MESH = pl.DeviceIdType.MESH
SUB = 8
STEPS = 2


def dot(left, right):
    return jnp.dot(left, right, preferred_element_type=F32)


def act(values):
    scale = lax.rsqrt(jnp.mean(values * values, axis=-1, keepdims=True) + EPSILON)
    half = values * (scale * 0.5)
    return half + half * jnp.tanh(half)


def shift_on(odd):
    rows = lax.broadcasted_iota(jnp.int32, odd.shape, 0)
    return jnp.where(rows == 0, 0.0, pltpu.roll(odd, 1, 0))


def shift_back(even):
    count = even.shape[0]
    rows = lax.broadcasted_iota(jnp.int32, even.shape, 0)
    return jnp.where(rows == count - 1, 0.0, pltpu.roll(even, count - 1, 0))


def kernel(
    rows_n,
    dims,
    times_ref,
    xin_ref,
    emb_ref,
    win_ref,
    wout_ref,
    stale_hbm,
    wenc_hbm,
    wdown_hbm,
    wtmid_hbm,
    wup_hbm,
    wskip_hbm,
    wdec_hbm,
    wtime_hbm,
    xo_ref,
    feat_ref,
    wenc,
    wdown,
    wtm,
    wup,
    wskip,
    wdec,
    wtime,
    inbuf,
    recvx,
    xs,
    xh,
    lift,
    mixs,
    enc,
    a3e,
    a3d,
    a3g,
    gs,
    gh,
    bs,
    bh,
    lows,
    qs,
    qr,
    taps,
    xcs,
    xch,
    raised,
    mun,
    fsend,
    bias_e,
    bias_m,
    bias_d,
    wsem,
    ssem,
    rsem,
):
    rd, cols, chans, mid = dims
    half = cols // 2
    hr = rd // 2
    seg = lax.axis_index("segment")
    row = lax.axis_index("rows")
    first = seg == 0
    has_up = row > 0
    has_dn = row < rows_n - 1
    up = jnp.maximum(row - 1, 0)
    dn = jnp.minimum(row + 1, rows_n - 1)
    pair = 1 - seg

    fetch = {
        "own": pltpu.make_async_copy(stale_hbm.at[seg], inbuf.at[seg], wsem.at[0]),
        "skip": pltpu.make_async_copy(wskip_hbm, wskip, wsem.at[1]),
        "time": pltpu.make_async_copy(wtime_hbm, wtime, wsem.at[2]),
        "enc": pltpu.make_async_copy(wenc_hbm, wenc, wsem.at[3]),
        "down": pltpu.make_async_copy(wdown_hbm, wdown, wsem.at[4]),
        "dec": pltpu.make_async_copy(wdec_hbm, wdec, wsem.at[5]),
        "tm_own": pltpu.make_async_copy(wtmid_hbm.at[1], wtm.at[0], wsem.at[6]),
        "tm_other": pltpu.make_async_copy(wtmid_hbm.at[2 * pair], wtm.at[1], wsem.at[7]),
        "up": pltpu.make_async_copy(wup_hbm, wup, wsem.at[8]),
    }
    for item in fetch.values():
        item.start()

    def remote(src, dst, index, where):
        return pltpu.make_async_remote_copy(
            src_ref=src,
            dst_ref=dst,
            send_sem=ssem.at[index],
            recv_sem=rsem.at[index],
            device_id=where,
            device_id_type=MESH,
        )

    to_pair, to_up, to_dn = {"segment": pair}, {"rows": up}, {"rows": dn}
    swap = remote(stale_hbm.at[pair], inbuf.at[seg], 0, to_pair)
    swapx = remote(xin_ref.at[pair], recvx, 1, to_pair)
    x_up = remote(xs.at[0], xh.at[1], 2, to_up)
    x_dn = remote(xs.at[rd - 1], xh.at[0], 3, to_dn)
    g_dn = [remote(gs.at[s], gh.at[s], 4 + 6 * s, to_dn) for s in range(STEPS)]
    b_up = [remote(bs.at[s, 0], bh.at[s, 1], 5 + 6 * s, to_up) for s in range(STEPS)]
    b_dn = [remote(bs.at[s, 1], bh.at[s, 0], 6 + 6 * s, to_dn) for s in range(STEPS)]
    q_sw = [remote(qs.at[s], qr.at[s], 7 + 6 * s, to_pair) for s in range(STEPS)]
    c_up = [remote(xcs.at[s, 0], xch.at[s, 1], 8 + 6 * s, to_up) for s in range(STEPS)]
    c_dn = [remote(xcs.at[s, 1], xch.at[s, 0], 9 + 6 * s, to_dn) for s in range(STEPS)]
    f_sw = [
        remote(
            fsend.at[pl.ds(h * hr, hr)],
            feat_ref.at[seg, pl.ds(h * hr, hr)],
            16 + h,
            to_pair,
        )
        for h in range(2)
    ]
    xo_sw = remote(xs, xo_ref.at[seg], 18, to_pair)

    def send_up(copy):
        pl.when(has_up)(copy.start)

    def send_dn(copy):
        pl.when(has_dn)(copy.start)

    barrier = pltpu.get_barrier_semaphore()
    pl.semaphore_signal(barrier, inc=1, device_id=to_pair, device_id_type=MESH)

    @pl.when(has_up)
    def _():
        pl.semaphore_signal(barrier, inc=1, device_id=to_up, device_id_type=MESH)

    @pl.when(has_dn)
    def _():
        pl.semaphore_signal(barrier, inc=1, device_id=to_dn, device_id_type=MESH)

    pl.semaphore_wait(barrier, 1 + has_up.astype(jnp.int32) + has_dn.astype(jnp.int32))
    swap.start()
    swapx.start()

    @pl.when(jnp.logical_not(has_up))
    def _():
        xh[0] = jnp.zeros_like(xh[0])
        for s in range(STEPS):
            gh[s] = jnp.zeros_like(gh[s])
            bh[s, 0] = jnp.zeros_like(bh[s, 0])
            xch[s, 0] = jnp.zeros_like(xch[s, 0])

    @pl.when(jnp.logical_not(has_dn))
    def _():
        xh[1] = jnp.zeros_like(xh[1])
        for s in range(STEPS):
            bh[s, 1] = jnp.zeros_like(bh[s, 1])
            xch[s, 1] = jnp.zeros_like(xch[s, 1])

    def spread(ref, index, values):
        even, odd = values[:half], values[half:]
        even16, odd16 = even.astype(BF16), odd.astype(BF16)
        ref[index, :half, 0:chans] = shift_on(odd).astype(BF16)
        ref[index, half:, 0:chans] = even16
        ref[index, :half, chans : 2 * chans] = even16
        ref[index, half:, chans : 2 * chans] = odd16
        ref[index, :half, 2 * chans :] = odd16
        ref[index, half:, 2 * chans :] = shift_back(even).astype(BF16)

    def spread_down(step, index, values):
        even, odd = values[:half], values[half:]
        a3g[step, index, :, 0:chans] = shift_on(odd).astype(BF16)
        a3g[step, index, :, chans : 2 * chans] = even.astype(BF16)
        a3g[step, index, :, 2 * chans :] = odd.astype(BF16)

    def lift_row(x_row):
        return lax.dot_general(
            x_row.astype(BF16),
            win_ref[...],
            (((0,), (0,)), ((), ())),
            preferred_element_type=F32,
        )

    def enc_front():
        def one(r, carry):
            lifted = lift_row(xs[r])
            lift[r] = lifted
            spread(a3e, r + 1, act(lifted))
            return carry

        lax.fori_loop(0, rd, one, 0)

    def gate_rows(step):
        def one(r, carry):
            g = act(enc[r].astype(F32))
            spread_down(step, r + 1, g)

            @pl.when(r == rd - 1)
            def _():
                gs[step] = g.astype(BF16)

            return carry

        lax.fori_loop(0, rd, one, 0)
        send_dn(g_dn[step])

    def mix_rows(step):
        def one(r, carry):
            if step == 0:
                mixed = dot(inbuf[1, r], wskip[0]) + dot(enc[r], wskip[1])
            else:
                low = dot(raised[r // 2], wskip[0])
                mixed = jnp.concatenate([low, low], axis=0) + dot(enc[r], wskip[1])
            mixs[r] = mixed
            b = act(mixed)
            spread(a3d, r + 1, b)

            @pl.when(r == 0)
            def _():
                bs[step, 0] = b.astype(BF16)

            @pl.when(r == rd - 1)
            def _():
                bs[step, 1] = b.astype(BF16)

            return carry

        lax.fori_loop(0, rd, one, 0)
        send_up(b_up[step])
        send_dn(b_dn[step])

    def conv_half(a3, weight, h):
        total = None
        for dy in range(3):
            window = a3[h * hr + dy : h * hr + dy + hr].reshape(hr * cols, 3 * chans)
            part = dot(window, weight[dy])
            total = part if total is None else total + part
        return total

    def enc_half(step, h):
        base = lift[h * hr : (h + 1) * hr].reshape(hr * cols, chans)
        total = base + conv_half(a3e, wenc, h) + bias_e[step : step + 1]
        return total.astype(BF16).reshape(hr, cols, chans)

    def mid_front(step):
        spread_down(step, 0, gh[step].astype(F32))
        total = None
        for dy in range(3):
            window = jnp.concatenate([a3g[step, dy + 2 * i] for i in range(hr)], axis=0)
            part = dot(window, wdown[dy])
            total = part if total is None else total + part
        low = total + bias_m[step : step + 1]
        lows[...] = low
        qs[step] = act(low).astype(BF16)
        q_sw[step].start()

    def mid_tail(step):
        q_sw[step].wait_recv()
        total = lows[...] + dot(qs[step], wtm[0]) + dot(qr[step], wtm[1])
        lifted = dot(total.astype(BF16), wup[...]).astype(BF16)
        raised[...] = lifted.reshape(hr, half, chans)

    lane = lax.broadcasted_iota(jnp.int32, (SUB, cols), 1)

    def across(left, centre, right):
        before = jnp.where(
            lane < half,
            jnp.where(lane == 0, 0.0, pltpu.roll(left, half + 1, 1)),
            pltpu.roll(left, half, 1),
        )
        after = jnp.where(
            lane < half,
            pltpu.roll(right, half, 1),
            jnp.where(lane == cols - 1, 0.0, pltpu.roll(right, half - 1, 1)),
        )
        return before + centre + after

    def tap(r, k):
        return taps[r, k * SUB : (k + 1) * SUB]

    def coefficient(step):
        return (jnp.full((SUB, cols), times_ref[step]).astype(F32) + 1.0) / 1000.0

    def dec(step):
        pl.when(has_dn)(b_up[step].wait_recv)
        pl.when(has_up)(b_dn[step].wait_recv)
        spread(a3d, 0, bh[step, 0].astype(F32))
        spread(a3d, rd + 1, bh[step, 1].astype(F32))
        for h in range(2):
            base = mixs[h * hr : (h + 1) * hr].reshape(hr * cols, chans)
            total = base + conv_half(a3d, wdec, h) + bias_d[step : step + 1]
            o = act(total).astype(BF16)
            for i in range(hr):
                taps[h * hr + i] = lax.dot_general(
                    wout_ref[...],
                    o[i * cols : (i + 1) * cols],
                    (((1,), (1,)), ((), ())),
                    preferred_element_type=F32,
                )
        coef = coefficient(step)
        for r in range(rd):
            sums = []
            for dx in range(3):
                parts = [tap(r + dy - 1, dy * 3 + dx) for dy in range(3) if 0 <= r + dy - 1 < rd]
                sums.append(functools.reduce(jnp.add, parts))
            xs[r] = xs[r] - coef * across(*sums)
        xcs[step, 0, 0] = xs[0]
        xcs[step, 0, 1] = coef * across(tap(0, 6), tap(0, 7), tap(0, 8))
        xcs[step, 1, 0] = xs[rd - 1]
        xcs[step, 1, 1] = coef * across(tap(rd - 1, 0), tap(rd - 1, 1), tap(rd - 1, 2))
        send_up(c_up[step])
        send_dn(c_dn[step])

    def finish_x(step):
        pl.when(has_dn)(c_up[step].wait_recv)
        pl.when(has_up)(c_dn[step].wait_recv)
        xs[0] = xs[0] - xch[step, 0, 1]
        xs[rd - 1] = xs[rd - 1] - xch[step, 1, 1]

    swapx.wait_recv()
    xs[...] = xin_ref[seg] + recvx[...]
    send_up(x_up)
    send_dn(x_dn)
    enc_front()

    at = lax.broadcasted_iota(jnp.int32, (cols, cols), 0)
    col = lax.broadcasted_iota(jnp.int32, (cols, cols), 1)
    source = jnp.where(at < half, 2 * at, 2 * (at - half) + 1)
    sort = jnp.where(col == source, 1.0, 0.0).astype(BF16)
    fetch["own"].wait()
    swap.wait_recv()

    def arrange(r, carry):
        enc[r] = dot(sort, inbuf[0, r]).astype(BF16)
        inbuf[1, r] = dot(sort, inbuf[1, r]).astype(BF16)
        return carry

    lax.fori_loop(0, rd, arrange, 0)
    gate_rows(0)
    fetch["skip"].wait()
    mix_rows(0)

    fetch["time"].wait()
    bias = dot(emb_ref[...], wtime[...])
    bias_e[...] = bias[:, :chans]
    bias_m[...] = bias[:, chans : chans + mid]
    bias_d[...] = bias[:, chans + mid :]

    pl.when(has_dn)(x_up.wait_recv)
    pl.when(has_up)(x_dn.wait_recv)
    spread(a3e, 0, act(lift_row(xh[0])))
    spread(a3e, rd + 1, act(lift_row(xh[1])))
    pl.when(has_up)(x_up.wait_send)
    pl.when(has_dn)(x_dn.wait_send)
    fetch["enc"].wait()
    for h in range(2):
        enc[h * hr : (h + 1) * hr] = enc_half(0, h)
    gate_rows(1)
    fetch["down"].wait()
    pl.when(has_up)(g_dn[0].wait_recv)
    mid_front(0)
    fetch["dec"].wait()
    dec(0)
    fetch["tm_own"].wait()
    fetch["tm_other"].wait()
    fetch["up"].wait()
    mid_tail(0)

    mix_rows(1)
    pl.when(has_up)(g_dn[1].wait_recv)
    mid_front(1)
    finish_x(0)
    enc_front()
    above = xch[0, 0, 0] - xcs[0, 0, 1]
    below = xch[0, 1, 0] - xcs[0, 1, 1]
    above = above * jnp.full(above.shape, has_up.astype(jnp.int32)).astype(F32)
    below = below * jnp.full(below.shape, has_dn.astype(jnp.int32)).astype(F32)
    spread(a3e, 0, act(lift_row(above)))
    spread(a3e, rd + 1, act(lift_row(below)))
    dec(1)
    mid_tail(1)

    at2 = lax.broadcasted_iota(jnp.int32, (cols, half), 0)
    col2 = lax.broadcasted_iota(jnp.int32, (cols, half), 1)
    twice = jnp.where(col2 == at2 // 2, 1.0, 0.0).astype(BF16)
    target = jnp.where(col < half, 2 * col, 2 * (col - half) + 1)
    unsort = jnp.where(at == target, 1.0, 0.0).astype(BF16)
    for i in range(hr):
        wide = dot(twice, raised[i]).astype(BF16)
        mun[2 * i] = wide
        mun[2 * i + 1] = wide
    for h in range(2):
        fresh = enc_half(1, h)
        plain = [dot(unsort, fresh[i]).astype(BF16) for i in range(hr)]

        @pl.when(first)
        def _():
            for i in range(hr):
                feat_ref[0, h * hr + i] = plain[i]
                fsend[h * hr + i] = mun[h * hr + i]

        @pl.when(jnp.logical_not(first))
        def _():
            for i in range(hr):
                feat_ref[1, h * hr + i] = mun[h * hr + i]
                fsend[h * hr + i] = plain[i]

        f_sw[h].start()
        if h == 0:
            finish_x(1)
            xo_ref[seg] = xs[...]
            xo_sw.start()

    swap.wait_send()
    swapx.wait_send()
    for s in range(STEPS):
        pl.when(has_dn)(g_dn[s].wait_send)
        pl.when(has_up)(b_up[s].wait_send)
        pl.when(has_dn)(b_dn[s].wait_send)
        q_sw[s].wait_send()
        pl.when(has_up)(c_up[s].wait_send)
        pl.when(has_dn)(c_dn[s].wait_send)
    for copy in (*f_sw, xo_sw):
        copy.wait()


def body(rows_n, latent, stale, timesteps, w_in, w_enc, w_down, w_tmid, w_up, w_skip, w_dec, w_out, w_time):
    frames, rd, merged = latent.shape
    cols, chans = stale.shape[3], stale.shape[4]
    mid = w_down.shape[3]
    lat = w_in.shape[0]
    segs = cols * lat // merged
    half, hr = cols // 2, rd // 2
    part = half // segs
    seg = lax.axis_index("segment")

    pieces = latent.reshape(frames, rd, part, 2, lat).transpose(0, 1, 4, 3, 2)
    mine = (jnp.arange(segs) == seg)[None, None, None, None, :, None]
    xin = jnp.where(mine, pieces[:, :, :, :, None, :], 0.0).reshape(frames, rd, lat, cols)
    xin = jnp.pad(xin, ((0, 0), (0, 0), (0, SUB - lat), (0, 0)))

    quarter = w_time.shape[0] // 2
    freqs = jnp.exp(-math.log(10000.0) * jnp.arange(quarter).astype(F32) / quarter)
    angles = timesteps.astype(F32)[:, None] * freqs
    emb = jax.nn.silu(jnp.concatenate([jnp.sin(angles), jnp.cos(angles)], axis=1)).astype(BF16)
    emb = jnp.pad(emb, ((0, 16 - emb.shape[0]), (0, 0)))

    win = jnp.pad(w_in, ((0, SUB - lat), (0, 0)))
    wout = jnp.pad(w_out.transpose(0, 1, 3, 2), ((0, 0), (0, 0), (0, SUB - lat), (0, 0)))
    wout = wout.reshape(9 * SUB, chans)

    vmem = pl.BlockSpec(memory_space=pltpu.VMEM)
    anywhere = pl.BlockSpec(memory_space=pl.ANY)
    rowed = (rd, cols, chans)
    xo, feat = pl.pallas_call(
        functools.partial(kernel, rows_n, (rd, cols, chans, mid)),
        out_shape=(
            jax.ShapeDtypeStruct((frames, rd, SUB, cols), F32),
            jax.ShapeDtypeStruct((frames, *rowed), BF16),
        ),
        in_specs=[pl.BlockSpec(memory_space=pltpu.SMEM)] + [vmem] * 4 + [anywhere] * 8,
        out_specs=(vmem, vmem),
        scratch_shapes=[
            pltpu.VMEM((3, 3 * chans, chans), BF16),
            pltpu.VMEM((3, 3 * chans, mid), BF16),
            pltpu.VMEM((2, mid, mid), BF16),
            pltpu.VMEM((mid, chans), BF16),
            pltpu.VMEM((2, chans, chans), BF16),
            pltpu.VMEM((3, 3 * chans, chans), BF16),
            pltpu.VMEM(w_time.shape, BF16),
            pltpu.VMEM((2, *rowed), BF16),
            pltpu.VMEM((rd, SUB, cols), F32),
            pltpu.VMEM((rd, SUB, cols), F32),
            pltpu.VMEM((2, SUB, cols), F32),
            pltpu.VMEM(rowed, F32),
            pltpu.VMEM(rowed, F32),
            pltpu.VMEM(rowed, BF16),
            pltpu.VMEM((rd + 2, cols, 3 * chans), BF16),
            pltpu.VMEM((rd + 2, cols, 3 * chans), BF16),
            pltpu.VMEM((STEPS, rd + 1, half, 3 * chans), BF16),
            pltpu.VMEM((STEPS, cols, chans), BF16),
            pltpu.VMEM((STEPS, cols, chans), BF16),
            pltpu.VMEM((STEPS, 2, cols, chans), BF16),
            pltpu.VMEM((STEPS, 2, cols, chans), BF16),
            pltpu.VMEM((hr * half, mid), F32),
            pltpu.VMEM((STEPS, hr * half, mid), BF16),
            pltpu.VMEM((STEPS, hr * half, mid), BF16),
            pltpu.VMEM((rd, 9 * SUB, cols), F32),
            pltpu.VMEM((STEPS, 2, 2, SUB, cols), F32),
            pltpu.VMEM((STEPS, 2, 2, SUB, cols), F32),
            pltpu.VMEM((hr, half, chans), BF16),
            pltpu.VMEM(rowed, BF16),
            pltpu.VMEM(rowed, BF16),
            pltpu.VMEM((16, chans), F32),
            pltpu.VMEM((16, mid), F32),
            pltpu.VMEM((16, chans), F32),
            pltpu.SemaphoreType.DMA((9,)),
            pltpu.SemaphoreType.DMA((19,)),
            pltpu.SemaphoreType.DMA((19,)),
        ],
        compiler_params=pltpu.CompilerParams(
            collective_id=0, has_side_effects=True, vmem_limit_bytes=56 * 2**20
        ),
    )(
        timesteps,
        xin,
        emb,
        win,
        wout,
        stale[0],
        w_enc.reshape(3, 3 * chans, chans),
        w_down.reshape(3, 3 * chans, mid),
        w_tmid,
        w_up,
        w_skip.reshape(2, chans, chans),
        w_dec.reshape(3, 3 * chans, chans),
        w_time,
    )
    whole = xo[:, :, :lat].reshape(frames, rd, lat, 2, segs, part)
    own = lax.dynamic_index_in_dim(whole, seg, axis=4, keepdims=False)
    result = own.transpose(0, 1, 4, 3, 2).reshape(frames, rd, merged)
    return (result, feat[None])


def solution(mesh):
    placed = (
        P("clips", "rows", "segment"),
        P("segment", "clips", "rows", None, None),
        P("clips"),
        P(),
        P(),
        P(),
        P(),
        P(),
        P(),
        P(),
        P(),
        P(),
    )
    return jax.shard_map(
        functools.partial(body, mesh.shape["rows"]),
        mesh=mesh,
        in_specs=placed,
        out_specs=(P("clips", "rows", "segment"), P("segment", "clips", "rows", None, None)),
        check_vma=False,
    )
```
